32 devices in a mesh: seq: 16 (over z, y, core), ch: 2 (over x).
Axes of the slice: x: 2, y: 2, z: 4, core: 2. Of those that a mesh axis runs over, the one named last changes fastest.
Arguments:
- grad_out: bfloat16 [4096, 4096], P('seq', 'ch'), may hold values from -6 to 6
- saved_in: bfloat16 [4096, 4096], P('seq', 'ch'), may hold values from -6 to 6
- filter_taps: bfloat16 [256, 4096], P(None, 'ch'), may hold values from -0.375 to 0.375
- skip_gain: float32 [4096], P('ch'), may hold values from 0.5 to 1.5
- projection: bfloat16 [4096, 4096], P('seq', 'ch'), may hold values from -0.09375 to 0.09375
Outputs:
- grad_in: bfloat16 [4096, 4096], P('seq', 'ch')
- filter_grad: float32 [256, 4096], P('seq', 'ch')
The draws below stay inside these ranges and needn't reach their ends.
All inputs are finite; a program needn't handle non-finite values.
Results may differ from the reference program's by a relative error of at most 0.015.
Values may be sent and summed in bfloat16 or wider, within the bound.
No kernel may reach another device: no remote copies, remote signals or barrier semaphores. Data moves between devices by JAX's collectives and lax.ppermute only.
A program may use at most 64 MiB of HBM per device.

```python
import jax
import jax.numpy as jnp
from jax import lax

D = 4096
FILTER = 256
TOKENS = 4096
N_CH = 2


def block_levels(key, shape, cuts, smallest, high):
    gain, own = 1.0, jax.random.fold_in(key, 6)
    for position, parts in cuts:
        draws = jnp.exp(jax.random.uniform(jax.random.fold_in(own, position), (parts,), jnp.float32, smallest / len(cuts), high / len(cuts)))
        gain = gain * jnp.repeat(draws, shape[position] // parts).reshape([-1 if axis == position else 1 for axis in range(len(shape))])
    return gain


def centred(rng, shape, deviation, bound, pieces=(), held_as=jnp.bfloat16):
    array = jax.random.normal(rng, shape, jnp.float32) * deviation
    if len(pieces) > 0:
        array = block_levels(rng, shape, pieces, -0.22, 0.18) * array
    return jnp.clip(array, min=-bound, max=bound).astype(held_as)


def setup_inputs(seed: int = 0) -> dict:
    key_of = jax.random.split(jax.random.key(seed), 6)
    return {
        "grad_out": centred(key_of[0], (TOKENS, D), 1.0, 6.0, ((0, 16), (1, 2))),
        "saved_in": centred(key_of[1], (TOKENS, D), 1.0, 6.0, ((0, 16), (1, 2))),
        "filter_taps": centred(key_of[2], (FILTER, D), FILTER ** -0.5, 0.375, ((1, 2),)),
        "skip_gain": jnp.clip(0.5 + 1.0 * jax.random.uniform(key_of[3], (D,), jnp.float32) ** block_levels(key_of[3], (D,), ((0, 2),), -0.2, 0.2), 0.5, 1.5),
        "projection": centred(key_of[4], (D, D), D ** -0.5, 0.09375, ((0, 16), (1, 2))),
    }


def spectral(first, second, offset, count):
    fft_size = 1
    while fft_size < first.shape[0] + second.shape[0]:
        fft_size = fft_size * 2
    first_hat = jnp.fft.rfft(first, n=fft_size, axis=0)
    second_hat = jnp.fft.rfft(second, n=fft_size, axis=0)
    linear = jnp.fft.irfft(first_hat * second_hat, n=fft_size, axis=0)
    return linear[offset:offset + count]

def reference(grad_out, saved_in, filter_taps, skip_gain, projection):
    tap_count = filter_taps.shape[0]
    seq_length = grad_out.shape[0]
    gradient = grad_out.astype(jnp.float32)
    inputs = saved_in.astype(jnp.float32)
    taps = filter_taps.astype(jnp.float32)
    reversed_taps = taps[:, ::-1]
    block_width = min(512, D)
    conv_blocks = []
    forward_blocks = []
    mirror_blocks = []
    for block_index in range(D // block_width):
        low = block_index * block_width
        high = low + block_width
        grad_block = gradient[:, low:high]
        input_block = inputs[:, low:high]
        forward = spectral(grad_block, taps[::-1, low:high], tap_count - 1, seq_length)
        backward = spectral(grad_block, reversed_taps[:, low:high], 0, seq_length)
        conv_blocks.append(forward + backward)
        forward_blocks.append(spectral(grad_block, input_block[::-1], seq_length - 1, tap_count))
        mirror_blocks.append(spectral(input_block, grad_block[::-1], seq_length - 1, tap_count))
    conv_sum = jnp.concatenate(conv_blocks, axis=1)
    filter_sum = jnp.concatenate(forward_blocks, axis=1) + jnp.concatenate(mirror_blocks, axis=1)[:, ::-1]
    grad_conv = (conv_sum + skip_gain[None, :] * gradient).astype(jnp.bfloat16)
    shard_width = D // N_CH
    total = jnp.zeros((seq_length, D), jnp.float32)
    for shard_index in range(N_CH):
        low = shard_index * shard_width
        high = low + shard_width
        partial_value = jnp.dot(grad_conv[:, low:high], projection[:, low:high].T, preferred_element_type=jnp.float32)
        rounded = lax.optimization_barrier(partial_value.astype(jnp.bfloat16))
        total = total + rounded.astype(jnp.float32)
    grad_in = total.astype(jnp.bfloat16)
    filter_grad = filter_sum * (1.0 / jnp.sqrt(jnp.float32(TOKENS)))
    return (grad_in, filter_grad)
```

```python
import math

import jax
import jax.numpy as jnp
import numpy as np
from jax import lax
from jax.experimental import pallas as pl
from jax.experimental.pallas import tpu as pltpu
from jax.sharding import PartitionSpec as P

INNER = 4
F32, BF16 = jnp.float32, jnp.bfloat16
VMEM = pl.BlockSpec(memory_space=pltpu.VMEM)
ANY = pl.BlockSpec(memory_space=pl.ANY)
MIB = 1 << 20
SMALL = pl.CostEstimate(flops=1000, bytes_accessed=1000, transcendentals=0)


def cost(us):
    return pl.CostEstimate(flops=int(us * 1e9), bytes_accessed=int(us * 1e6), transcendentals=0)


def params(mib):
    return pltpu.CompilerParams(vmem_limit_bytes=mib * MIB)


def shape(dims, dtype):
    return jax.ShapeDtypeStruct(dims, dtype)


def swap_seq(value, k):
    count = lax.axis_size("seq")
    return lax.ppermute(value, "seq", [(i, i ^ k) for i in range(count)])


def mirror_ch(value):
    count = lax.axis_size("ch")
    return lax.ppermute(value, "ch", [(i, count - 1 - i) for i in range(count)])


def group_index():
    return lax.rem(lax.axis_index("seq"), INNER)


def columns(block, width):
    return pl.ds(pl.multiple_of(block * width, width), width)


def dot(a, b):
    return jnp.dot(a, b, preferred_element_type=F32)


def dot_nt(a, b):
    return lax.dot_general(a, b, (((1,), (1,)), ((), ())), preferred_element_type=F32)


BLOCKS = INNER + 2
PAIRS = BLOCKS // 2


def angles(j):
    return [2 * math.pi * (j + 0.5) * b / BLOCKS for b in range(BLOCKS)]


def exact(value):
    return 0.0 if abs(value) < 1e-9 else float(value)


def transforms(rows):
    window = BLOCKS * rows
    into, at_taps = [], []
    for j in range(PAIRS):
        upper, lower = [], []
        for index, sign in ((j, 1.0), (BLOCKS - 1 - j, -1.0)):
            k = np.arange(index, window // 2, BLOCKS)
            angle = 2 * np.pi * (k + 0.5)[:, None] * np.arange(rows)[None, :] / window
            c, s = np.cos(angle), np.sin(angle)
            upper += [np.concatenate([c, sign * s], 1), np.concatenate([-s, sign * c], 1)]
            lower += [c, s]
        into.append(np.concatenate(upper, 0))
        at_taps.append(np.concatenate(lower, 0))
    into, at_taps = np.stack(into), np.stack(at_taps)
    cast = lambda a: np.ascontiguousarray(a).astype(np.float32).astype(BF16)
    turn = lambda a: a.transpose(0, 2, 1)
    return {
        "into": cast(into),
        "back": cast(turn(into)),
        "taps": cast(at_taps),
        "lags": cast(turn(at_taps)),
    }


def reversal(count):
    return np.eye(count, dtype=np.float32)[::-1].astype(BF16)


def tie(value, *deps):
    def kernel(*refs):
        pass

    return pl.pallas_call(
        kernel,
        out_shape=shape(value.shape, value.dtype),
        in_specs=[ANY] * (1 + len(deps)),
        out_specs=ANY,
        input_output_aliases={0: 0},
        cost_estimate=SMALL,
        name="tie",
    )(value, *deps)


def quarters(value, deps=(), mirror=None):
    rows, width = value.shape
    cq = width // INNER
    n_in = 1 + (mirror is not None)

    def kernel(*refs):
        q = group_index()
        outs = refs[n_in + len(deps) :]
        for k in range(INNER):
            outs[k][...] = refs[0][:, columns(q ^ k, cq)]
        if mirror is not None:
            outs[INNER][...] = refs[1][:, columns(INNER - 1 - q, cq)]

    out_shape = [shape((rows, cq), value.dtype)] * INNER
    inputs = [value]
    if mirror is not None:
        inputs.append(mirror)
        out_shape.append(shape((mirror.shape[0], cq), mirror.dtype))
    return pl.pallas_call(
        kernel,
        out_shape=out_shape,
        in_specs=[VMEM] * n_in + [ANY] * len(deps),
        out_specs=[VMEM] * len(out_shape),
        compiler_params=params(16),
        cost_estimate=cost(1),
        name="quarters",
    )(*inputs, *deps)


def halves_of_quarters(value, deps):
    rows, width = value.shape
    cq = width // INNER

    def kernel(*refs):
        q = group_index()
        own, near, far = refs[1 + len(deps) :]
        own[...] = refs[0][:, columns(q, cq)]
        near[...] = refs[0][:, columns(q ^ 1, cq)]
        far[0] = refs[0][:, columns(q ^ 2, cq)]
        far[1] = refs[0][:, columns(q ^ 3, cq)]

    dims = [(rows, cq), (rows, cq), (2, rows, cq)]
    return pl.pallas_call(
        kernel,
        out_shape=[shape(d, value.dtype) for d in dims],
        in_specs=[VMEM] + [ANY] * len(deps),
        out_specs=[VMEM] * 3,
        compiler_params=params(16),
        cost_estimate=cost(1),
        name="halves_of_quarters",
    )(value, *deps)


def spread(pieces):
    return [pieces[0]] + [swap_seq(pieces[k], k) for k in range(1, INNER)]


def combined(blocks, first, j):
    re, im = 0.0, 0.0
    for i, block in enumerate(blocks):
        angle = angles(j)[first + i]
        c, s = exact(math.cos(angle)), exact(-math.sin(angle))
        if c:
            re = re + c * block
        if s:
            im = im + s * block
    return jnp.concatenate([re.astype(BF16), im.astype(BF16)], 0)


def complex_rows(value, n):
    return [(value[2 * i * n : (2 * i + 1) * n], value[(2 * i + 1) * n : (2 * i + 2) * n]) for i in range(2)]


def chunk_of(cq):
    return min(256, cq)


def filtered(pieces, before, after, own_taps, mirrored, gain, const, deps):
    rows, cq = pieces[0].shape
    taps = own_taps.shape[0]
    chunk = chunk_of(cq)
    n = rows // 2
    scale = 2.0 / (BLOCKS * rows)

    def kernel(*refs):
        before_ref, after_ref, taps_ref, mirror_ref, gain_ref, into, back, at_taps = refs[INNER : INNER + 8]
        spectrum, conv, ordered = refs[INNER + 8 + len(deps) :]
        q = group_index()
        for k in range(INNER):
            ordered[q ^ k] = refs[k][...].astype(F32)
        blocks = [before_ref[...].astype(F32)] + [ordered[i] for i in range(INNER)] + [after_ref[...].astype(F32)]
        direct = gain_ref[...]
        outs = [0.0] * INNER
        for j in range(PAIRS):
            g = dot(into[j], combined(blocks, 0, j))
            spectrum[j] = g.astype(BF16)
            own, other = dot(at_taps[j], taps_ref[...]), dot(at_taps[j], mirror_ref[...])
            product = []
            for (gr, gi), (ar, ai), (br, bi) in zip(
                complex_rows(g, n), complex_rows(own, n), complex_rows(other, n)
            ):
                hr, hi = (ar + br + direct) * scale, (ai - bi) * scale
                product += [(gr * hr - gi * hi).astype(BF16), (gr * hi + gi * hr).astype(BF16)]
            w = dot(back[j], jnp.concatenate(product, 0))
            for i in range(INNER):
                angle = angles(j)[i + 1]
                c, s = exact(math.cos(angle)), exact(-math.sin(angle))
                if c:
                    outs[i] = outs[i] + c * w[:rows]
                if s:
                    outs[i] = outs[i] + s * w[rows:]
        for i in range(INNER):
            conv[i * rows : (i + 1) * rows, :] = outs[i].astype(BF16)

    cols = lambda r: pl.BlockSpec((r, chunk), lambda i: (0, i))
    whole = lambda a: pl.BlockSpec(a.shape, lambda i: (0, 0, 0))
    return pl.pallas_call(
        kernel,
        grid=(cq // chunk,),
        out_shape=[shape((PAIRS, 2 * rows, cq), BF16), shape((INNER * rows, cq), BF16)],
        in_specs=[cols(rows)] * (INNER + 2)
        + [cols(taps)] * 2
        + [cols(1)]
        + [whole(const["into"]), whole(const["back"]), whole(const["taps"])]
        + [ANY] * len(deps),
        out_specs=[pl.BlockSpec((PAIRS, 2 * rows, chunk), lambda i: (0, 0, i)), cols(INNER * rows)],
        scratch_shapes=[pltpu.VMEM((INNER, rows, chunk), F32)],
        compiler_params=params(32),
        cost_estimate=cost(6),
        name="filtered",
    )(*pieces, before, after, own_taps, mirrored, gain, const["into"], const["back"], const["taps"], *deps)


def correlations(pieces, spectrum, const, scale, deps):
    rows, cq = pieces[0].shape
    taps = const["lags"].shape[1]
    chunk = chunk_of(cq)
    n = rows // 2
    chunks = cq // chunk

    def kernel(*refs):
        spec, into, lags, flip = refs[INNER : INNER + 4]
        forward, turned, ordered = refs[INNER + 4 + len(deps) :]
        q = group_index()
        for k in range(INNER):
            ordered[q ^ k] = refs[k][...].astype(F32)
        blocks = [ordered[i] for i in range(INNER)]
        even, odd = 0.0, 0.0
        for j in range(PAIRS):
            x = dot(into[j], combined(blocks, 1, j))
            g = spec[j].astype(F32)
            for i, ((xr, xi), (gr, gi)) in enumerate(zip(complex_rows(x, n), complex_rows(g, n))):
                z_re = ((gr * xr + gi * xi) * scale).astype(BF16)
                z_im = ((gi * xr - gr * xi) * scale).astype(BF16)
                even += dot(lags[j, :, 2 * i * n : (2 * i + 1) * n], z_re)
                odd += dot(lags[j, :, (2 * i + 1) * n : (2 * i + 2) * n], z_im)
        forward[...] = even - odd
        turned[...] = dot((even + odd).astype(BF16), flip[...]).astype(BF16)

    cols = lambda r: pl.BlockSpec((r, chunk), lambda i: (0, i))
    whole = lambda a: pl.BlockSpec(a.shape, lambda i: (0, 0, 0))
    return pl.pallas_call(
        kernel,
        grid=(chunks,),
        out_shape=[shape((taps, cq), F32), shape((taps, cq), BF16)],
        in_specs=[cols(rows)] * INNER
        + [pl.BlockSpec((PAIRS, 2 * rows, chunk), lambda i: (0, 0, i))]
        + [whole(const["into"]), whole(const["lags"]), pl.BlockSpec((chunk, chunk), lambda i: (0, 0))]
        + [ANY] * len(deps),
        out_specs=[cols(taps), pl.BlockSpec((taps, chunk), lambda i: (0, chunks - 1 - i))],
        scratch_shapes=[pltpu.VMEM((INNER, rows, chunk), F32)],
        compiler_params=params(32),
        cost_estimate=cost(5),
        name="correlations",
    )(*pieces, spectrum, const["into"], const["lags"], reversal(chunk), *deps)


def own_quarter(filter_taps, mirrored, gain):
    taps, width = filter_taps.shape
    cq = width // INNER

    def kernel(taps_ref, mirror_ref, gain_ref, flip, taps_out, mirror_out, gain_out):
        at = columns(group_index(), cq)
        taps_out[...] = taps_ref[:, at]
        gain_out[...] = gain_ref[:, at]
        mirror_out[...] = dot(mirror_ref[...], flip[...]).astype(BF16)

    return pl.pallas_call(
        kernel,
        out_shape=[shape((taps, cq), BF16), shape((taps, cq), BF16), shape((1, cq), F32)],
        in_specs=[VMEM] * 4,
        out_specs=[VMEM] * 3,
        compiler_params=params(16),
        cost_estimate=cost(1),
        name="own_quarter",
    )(filter_taps, mirrored, gain, reversal(cq))


def project(conv, choices, dtype, deps=()):
    span, cq = conv[0].shape
    o_rows, width = choices[0][1].shape
    tile = span // INNER

    def kernel(*refs):
        blocks = refs[INNER : INNER + len(choices)]
        out, rhs, sem = refs[INNER + len(choices) + len(deps) :]
        q = group_index()
        z = lax.div(lax.axis_index("seq"), INNER)
        early = lax.axis_index("ch") == lax.div(z, 2)
        at_end = (z == 0) | (z == 3)
        holds = {
            "early": early,
            "late": jnp.logical_not(early),
            "early_end": early & at_end,
            "early_mid": early & jnp.logical_not(at_end),
            "late_end": jnp.logical_not(early) & at_end,
            "late_mid": jnp.logical_not(early | at_end),
        }

        @pl.when(pl.program_id(0) == 0)
        def _():
            for (condition, _), block in zip(choices, blocks):
                @pl.when(holds[condition])
                def _():
                    copy = pltpu.make_async_copy(block, rhs, sem)
                    copy.start()
                    copy.wait()

        total = 0.0
        for k in range(INNER):
            total += dot_nt(refs[k][...], rhs[:, columns(q ^ k, cq)])
        out[...] = total.astype(dtype)

    rows = pl.BlockSpec((tile, cq), lambda i: (i, 0))
    return pl.pallas_call(
        kernel,
        grid=(INNER,),
        out_shape=shape((span, o_rows), dtype),
        in_specs=[rows] * INNER + [ANY] * (len(choices) + len(deps)),
        out_specs=pl.BlockSpec((tile, o_rows), lambda i: (i, 0)),
        scratch_shapes=[pltpu.VMEM((o_rows, width), BF16), pltpu.SemaphoreType.DMA],
        compiler_params=params(24),
        cost_estimate=cost(3),
        name="project",
    )(*conv, *[block for _, block in choices], *deps)


def summed_rows(kept, got, dtype):
    span, width = kept.shape
    rows = span // INNER

    def kernel(kept_ref, got_ref, *outs):
        q = group_index()
        for k in range(INNER):
            at = pl.ds(pl.multiple_of((q ^ k) * rows, rows), rows)
            outs[k][...] = (kept_ref[at, :] + got_ref[at, :].astype(F32)).astype(dtype)

    return pl.pallas_call(
        kernel,
        out_shape=[shape((rows, width), dtype)] * INNER,
        in_specs=[VMEM] * 2,
        out_specs=[VMEM] * INNER,
        compiler_params=params(16),
        cost_estimate=cost(1),
        name="summed_rows",
    )(kept, got)


def assembled(rounds, width):
    rows, o_rows = rounds[0][0].shape

    def kernel(*refs):
        q = group_index()
        z = lax.div(lax.axis_index("seq"), INNER)
        out = refs[-1]
        for r in range(2):
            for k in range(INNER):
                block = (lax.rem(z, 2) ^ r) * INNER + (q ^ k)
                out[:, columns(block, o_rows)] = refs[r * INNER + k][...]

    return pl.pallas_call(
        kernel,
        out_shape=shape((rows, width), BF16),
        in_specs=[VMEM] * (2 * INNER),
        out_specs=VMEM,
        compiler_params=params(16),
        cost_estimate=cost(1),
        name="assembled",
    )(*rounds[0], *rounds[1])


def halved(kept, got, bit):
    count = kept.shape[0] // 4 if kept.ndim == 2 else kept.shape[1]
    cq = kept.shape[-1]

    def kernel(kept_ref, got_ref, keep_out, send_out):
        own = lax.rem(lax.div(lax.div(lax.axis_index("seq"), INNER), 1 << bit), 2)
        for side, out in ((own, keep_out), (1 - own, send_out)):
            if bit == 0:
                for high in range(2):
                    at = pl.ds(pl.multiple_of((2 * high + side) * count, count), count)
                    out[high] = (kept_ref[at, :] + got_ref[at, :].astype(F32)).astype(out.dtype)
            else:
                out[...] = (kept_ref[side] + got_ref[side].astype(F32)).astype(out.dtype)

    dims = (2, count, cq) if bit == 0 else (count, cq)
    return pl.pallas_call(
        kernel,
        out_shape=[shape(dims, F32), shape(dims, BF16)],
        in_specs=[VMEM] * 2,
        out_specs=[VMEM] * 2,
        compiler_params=params(8),
        cost_estimate=cost(1),
        name="halved",
    )(kept, got)


def side_by_side(pieces):
    rows, cq = pieces[0].shape

    def kernel(*refs):
        q = group_index()
        for k in range(INNER):
            refs[-1][:, columns(q ^ k, cq)] = refs[k][...]

    return pl.pallas_call(
        kernel,
        out_shape=shape((rows, INNER * cq), pieces[0].dtype),
        in_specs=[VMEM] * INNER,
        out_specs=VMEM,
        compiler_params=params(8),
        cost_estimate=cost(1),
        name="side_by_side",
    )(*pieces)


def placed_by_source(pieces, q):
    result = jnp.zeros((INNER,) + pieces[0].shape, pieces[0].dtype)
    for k, piece in enumerate(pieces):
        result = lax.dynamic_update_index_in_dim(result, piece, q ^ k, 0)
    return result


def by_member(value, q):
    return [lax.dynamic_index_in_dim(value, q ^ k, 0, keepdims=False) for k in range(INNER)]


def pick_member(pieces, q, member):
    result = pieces[0]
    for k in range(1, INNER):
        result = jnp.where((q ^ k) == member, pieces[k], result)
    return result


def body(grad_out, saved_in, filter_taps, skip_gain, projection):
    rows, width = grad_out.shape
    taps = filter_taps.shape[0]
    n_seq, n_ch = lax.axis_size("seq"), lax.axis_size("ch")
    outer = n_seq // INNER
    cq = width // INNER
    span = INNER * rows
    window = span + 2 * rows
    seq = lax.axis_index("seq")
    q, z = seq % INNER, seq // INNER
    const = transforms(rows)
    special = outer == 4 and n_ch == 2

    if special:
        shift = lambda v, table: lax.ppermute(
            v, "seq", [(INNER * a + i, INNER * b + i) for a, b in table for i in range(INNER)]
        )
        near = shift(projection, [(0, 1), (1, 0), (2, 3), (3, 2)])
        mid = shift(projection, [(1, 2), (2, 1)])

    *pieces, mirror_piece = quarters(grad_out, (), filter_taps)
    grads = spread(pieces)
    mirrored = mirror_ch(mirror_piece)
    quarter = own_quarter(filter_taps, mirrored, skip_gain.reshape(1, width))

    before = lax.ppermute(
        pick_member(grads, q, INNER - 1), "seq", [(i, i + INNER) for i in range(n_seq - INNER)]
    )
    after = lax.ppermute(
        pick_member(grads, q, 0), "seq", [(i + INNER, i) for i in range(n_seq - INNER)]
    )
    input_own, input_near, input_far = halves_of_quarters(saved_in, (grads[2],))
    input_far = swap_seq(input_far, 2)
    inputs = [input_own, swap_seq(input_near, 1), input_far[0], swap_seq(input_far[1], 1)]
    spectrum, conv = filtered(grads, before, after, *quarter, const, (input_far,))
    if special:
        near = tie(near, before, after)
        mid = tie(mid, before, after)
        far_ends = shift(mid, [(1, 0), (2, 3)])
        far_mid = shift(near, [(2, 1), (1, 2)])

    conv2 = swap_seq(conv, 2)
    conv1 = swap_seq(conv, 1)
    scale = 2.0 / window / math.sqrt(rows * n_seq)
    forward, turned = correlations(inputs, spectrum, const, scale, ())
    if special:
        conv2 = tie(conv2, far_mid, far_ends, turned)
    conv3 = swap_seq(conv2, 1)
    conv_parts = [conv, conv1, conv2, conv3]

    mirrored = lax.ppermute(
        turned,
        ("seq", "ch"),
        [
            (s * n_ch + c, (s ^ (INNER - 1)) * n_ch + n_ch - 1 - c)
            for s in range(n_seq)
            for c in range(n_ch)
        ],
    )
    if special:
        last = shift(far_mid, [(1, 0), (2, 3)])
        x2 = [("end", far_ends), ("mid", far_mid)]
        x3 = [("end", last), ("mid", mid)]
        sent = lambda late, soon: [("early_" + w, block) for w, block in late] + [("late", soon)]
        kept = lambda late, soon: [("late_" + w, block) for w, block in late] + [("early", soon)]
        first = project(conv_parts, sent(x2, projection), BF16)
        got = mirror_ch(first)
        forward = tie(forward, first)
        lag_kept, lag_sent = halved(forward, mirrored, 0)
        second = project(conv_parts, sent(x3, near), BF16)
        got2 = mirror_ch(second)
        own = project(conv_parts, kept(x2, projection), F32)
        own2 = project(conv_parts, kept(x3, near), F32)
        lag_kept, lag_sent = halved(lag_kept, swap_seq(lag_sent, INNER), 1)
        lag_pieces = summed_rows(lag_kept, swap_seq(lag_sent, 2 * INNER), F32)
        rounds = [spread(summed_rows(own, got, BF16)), spread(summed_rows(own2, got2, BF16))]
        grad_in = assembled(rounds, width)
    else:
        groups = [[INNER * a + i for a in range(outer)] for i in range(INNER)]
        proj_all = lax.all_gather(
            projection, "seq", axis=0, tiled=True, axis_index_groups=groups
        )
        conv_all = placed_by_source(conv_parts, q)
        partial_value = lax.dot_general(
            conv_all.transpose(1, 0, 2).reshape(span, width),
            proj_all,
            (((1,), (1,)), ((), ())),
            preferred_element_type=F32,
        )
        total = lax.psum_scatter(
            partial_value.astype(BF16), "ch", scatter_dimension=1, tiled=True
        )
        o_rows = projection.shape[0]
        moved = spread(by_member(total.reshape(INNER, rows, -1), q))
        stacked = placed_by_source(moved, q).reshape(INNER, rows, -1, o_rows)
        grad_in = stacked.transpose(1, 2, 0, 3).reshape(rows, width)

        groups = [[INNER * a + i for a in range(outer)] for i in range(INNER)]
        summed = lax.psum_scatter(
            forward + mirrored.astype(F32), "seq", scatter_dimension=0, tiled=True, axis_index_groups=groups
        )
        lag_pieces = by_member(summed.reshape(INNER, -1, cq), q)
    filter_grad = side_by_side(spread(lag_pieces))
    return (grad_in, filter_grad)


def solution(mesh):
    placed = (P("seq", "ch"), P("seq", "ch"), P(None, "ch"), P("ch"), P("seq", "ch"))
    return jax.shard_map(
        body,
        mesh=mesh,
        in_specs=placed,
        out_specs=(P("seq", "ch"), P("seq", "ch")),
        check_vma=False,
    )
```

```python
import math

import jax
import jax.numpy as jnp
import numpy as np
from jax import lax
from jax.experimental import pallas as pl
from jax.experimental.pallas import tpu as pltpu
from jax.sharding import PartitionSpec as P

INNER = 4
F32, BF16 = jnp.float32, jnp.bfloat16
VMEM = pl.BlockSpec(memory_space=pltpu.VMEM)
ANY = pl.BlockSpec(memory_space=pl.ANY)
HBM = pl.BlockSpec(memory_space=pltpu.HBM)
TOKEN = (8, 128)
MIB = 1 << 20
SMALL = pl.CostEstimate(flops=1000, bytes_accessed=1000, transcendentals=0)


def cost(us):
    return pl.CostEstimate(flops=int(us * 1e9), bytes_accessed=int(us * 1e6), transcendentals=0)


def params(mib):
    return pltpu.CompilerParams(vmem_limit_bytes=mib * MIB)


def shape(dims, dtype):
    return jax.ShapeDtypeStruct(dims, dtype)


def swap_seq(value, k):
    count = lax.axis_size("seq")
    return lax.ppermute(value, "seq", [(i, i ^ k) for i in range(count)])


def mirror_ch(value):
    count = lax.axis_size("ch")
    return lax.ppermute(value, "ch", [(i, count - 1 - i) for i in range(count)])


def group_index():
    return lax.rem(lax.axis_index("seq"), INNER)


def columns(block, width):
    return pl.ds(pl.multiple_of(block * width, width), width)


def dot(a, b):
    return jnp.dot(a, b, preferred_element_type=F32)


def dot_nt(a, b):
    return lax.dot_general(a, b, (((1,), (1,)), ((), ())), preferred_element_type=F32)


BLOCKS = INNER + 2
PAIRS = BLOCKS // 2


def angles(j):
    return [2 * math.pi * (j + 0.5) * b / BLOCKS for b in range(BLOCKS)]


def exact(value):
    return 0.0 if abs(value) < 1e-9 else float(value)


def transforms(rows):
    window = BLOCKS * rows
    into, at_taps = [], []
    for j in range(PAIRS):
        upper, lower = [], []
        for index, sign in ((j, 1.0), (BLOCKS - 1 - j, -1.0)):
            k = np.arange(index, window // 2, BLOCKS)
            angle = 2 * np.pi * (k + 0.5)[:, None] * np.arange(rows)[None, :] / window
            c, s = np.cos(angle), np.sin(angle)
            upper += [np.concatenate([c, sign * s], 1), np.concatenate([-s, sign * c], 1)]
            lower += [c, s]
        into.append(np.concatenate(upper, 0))
        at_taps.append(np.concatenate(lower, 0))
    into, at_taps = np.stack(into), np.stack(at_taps)
    cast = lambda a: np.ascontiguousarray(a).astype(np.float32).astype(BF16)
    turn = lambda a: a.transpose(0, 2, 1)
    return {
        "into": cast(into),
        "back": cast(turn(into)),
        "taps": cast(at_taps),
        "lags": cast(turn(at_taps)),
    }


def reversal(count):
    return np.eye(count, dtype=np.float32)[::-1].astype(BF16)


def tie(value, *deps):
    def kernel(value_ref, *rest):
        rest[-1][...] = value_ref[...]

    return pl.pallas_call(
        kernel,
        out_shape=shape(value.shape, value.dtype),
        in_specs=[VMEM] + [ANY] * len(deps),
        out_specs=VMEM,
        compiler_params=params(8),
        cost_estimate=cost(1),
        name="tie",
    )(value, *deps)


def quarters(value, outputs, deps=(), reverse=False):
    rows, width = value.shape
    cq = width // INNER
    total = sum(len(members) for members in outputs)

    def kernel(*refs):
        q = group_index()
        if reverse:
            q = INNER - 1 - q
        outs, sems = refs[1 + len(deps) : -1], refs[-1]
        copies = []
        for members, out in zip(outputs, outs):
            for i, k in enumerate(members):
                source = refs[0].at[:, columns(q ^ k, cq)]
                target = out if len(members) == 1 else out.at[i]
                copies.append(pltpu.make_async_copy(source, target, sems.at[len(copies)]))
        for copy in copies:
            copy.start()
        for copy in copies:
            copy.wait()

    dims = [(rows, cq) if len(m) == 1 else (len(m), rows, cq) for m in outputs]
    return pl.pallas_call(
        kernel,
        out_shape=[shape(d, value.dtype) for d in dims],
        in_specs=[HBM] + [ANY] * len(deps),
        out_specs=[ANY] * len(outputs),
        scratch_shapes=[pltpu.SemaphoreType.DMA((total,))],
        compiler_params=params(8),
        cost_estimate=cost(1),
        name="quarters",
    )(value, *deps)


def spread(pieces):
    return [pieces[0]] + [swap_seq(pieces[k], k) for k in range(1, INNER)]


def combined(blocks, first, j):
    re, im = 0.0, 0.0
    for i, block in enumerate(blocks):
        angle = angles(j)[first + i]
        c, s = exact(math.cos(angle)), exact(-math.sin(angle))
        if c:
            re = re + c * block
        if s:
            im = im + s * block
    return jnp.concatenate([re.astype(BF16), im.astype(BF16)], 0)


def complex_rows(value, n):
    return [(value[2 * i * n : (2 * i + 1) * n], value[(2 * i + 1) * n : (2 * i + 2) * n]) for i in range(2)]


def chunk_of(cq):
    return min(256, cq)


def filtered(pieces, before, after, own_taps, mirrored, gain, const, deps, large):
    rows, cq = pieces[0].shape
    taps = own_taps.shape[0]
    chunk = chunk_of(cq)
    n = rows // 2
    scale = 2.0 / (BLOCKS * rows)

    def kernel(*refs):
        before_ref, after_ref, taps_ref, mirror_ref, gain_ref, into, back, at_taps = refs[INNER : INNER + 8]
        spectrum, conv, ordered = refs[INNER + 8 + len(deps) + len(large) :]
        q = group_index()
        for k in range(INNER):
            ordered[q ^ k] = refs[k][...].astype(F32)
        blocks = [before_ref[...].astype(F32)] + [ordered[i] for i in range(INNER)] + [after_ref[...].astype(F32)]
        direct = gain_ref[...]
        outs = [0.0] * INNER
        for j in range(PAIRS):
            g = dot(into[j], combined(blocks, 0, j))
            spectrum[j] = g.astype(BF16)
            own, other = dot(at_taps[j], taps_ref[...]), dot(at_taps[j], mirror_ref[...])
            product = []
            for (gr, gi), (ar, ai), (br, bi) in zip(
                complex_rows(g, n), complex_rows(own, n), complex_rows(other, n)
            ):
                hr, hi = (ar + br + direct) * scale, (ai - bi) * scale
                product += [(gr * hr - gi * hi).astype(BF16), (gr * hi + gi * hr).astype(BF16)]
            w = dot(back[j], jnp.concatenate(product, 0))
            for i in range(INNER):
                angle = angles(j)[i + 1]
                c, s = exact(math.cos(angle)), exact(-math.sin(angle))
                if c:
                    outs[i] = outs[i] + c * w[:rows]
                if s:
                    outs[i] = outs[i] + s * w[rows:]
        for i in range(INNER):
            conv[i * rows : (i + 1) * rows, :] = outs[i].astype(BF16)

    cols = lambda r: pl.BlockSpec((r, chunk), lambda i: (0, i))
    whole = lambda a: pl.BlockSpec(a.shape, lambda i: (0, 0, 0))
    return pl.pallas_call(
        kernel,
        grid=(cq // chunk,),
        out_shape=[shape((PAIRS, 2 * rows, cq), BF16), shape((INNER * rows, cq), BF16)],
        in_specs=[cols(rows)] * (INNER + 2)
        + [cols(taps)] * 2
        + [cols(1)]
        + [whole(const["into"]), whole(const["back"]), whole(const["taps"])]
        + [ANY] * len(deps)
        + [HBM] * len(large),
        out_specs=[pl.BlockSpec((PAIRS, 2 * rows, chunk), lambda i: (0, 0, i)), cols(INNER * rows)],
        scratch_shapes=[pltpu.VMEM((INNER, rows, chunk), F32)],
        compiler_params=params(32),
        cost_estimate=cost(6),
        name="filtered",
    )(*pieces, before, after, own_taps, mirrored, gain, const["into"], const["back"], const["taps"], *deps, *large)


def correlations(pieces, spectrum, const, scale, deps):
    rows, cq = pieces[0].shape
    taps = const["lags"].shape[1]
    chunk = chunk_of(cq)
    n = rows // 2
    chunks = cq // chunk

    def kernel(*refs):
        spec, into, lags, flip = refs[INNER : INNER + 4]
        forward, turned, token, ordered = refs[INNER + 4 + len(deps) :]
        token[...] = jnp.zeros(TOKEN, F32)
        q = group_index()
        for k in range(INNER):
            ordered[q ^ k] = refs[k][...].astype(F32)
        blocks = [ordered[i] for i in range(INNER)]
        even, odd = 0.0, 0.0
        for j in range(PAIRS):
            x = dot(into[j], combined(blocks, 1, j))
            g = spec[j].astype(F32)
            for i, ((xr, xi), (gr, gi)) in enumerate(zip(complex_rows(x, n), complex_rows(g, n))):
                z_re = ((gr * xr + gi * xi) * scale).astype(BF16)
                z_im = ((gi * xr - gr * xi) * scale).astype(BF16)
                even += dot(lags[j, :, 2 * i * n : (2 * i + 1) * n], z_re)
                odd += dot(lags[j, :, (2 * i + 1) * n : (2 * i + 2) * n], z_im)
        forward[...] = even - odd
        turned[...] = dot((even + odd).astype(BF16), flip[...]).astype(BF16)

    cols = lambda r: pl.BlockSpec((r, chunk), lambda i: (0, i))
    whole = lambda a: pl.BlockSpec(a.shape, lambda i: (0, 0, 0))
    return pl.pallas_call(
        kernel,
        grid=(chunks,),
        out_shape=[shape((taps, cq), F32), shape((taps, cq), BF16), shape(TOKEN, F32)],
        in_specs=[cols(rows)] * INNER
        + [pl.BlockSpec((PAIRS, 2 * rows, chunk), lambda i: (0, 0, i))]
        + [whole(const["into"]), whole(const["lags"]), pl.BlockSpec((chunk, chunk), lambda i: (0, 0))]
        + [HBM] * len(deps),
        out_specs=[
            cols(taps),
            pl.BlockSpec((taps, chunk), lambda i: (0, chunks - 1 - i)),
            pl.BlockSpec(TOKEN, lambda i: (0, 0)),
        ],
        scratch_shapes=[pltpu.VMEM((INNER, rows, chunk), F32)],
        compiler_params=params(32),
        cost_estimate=cost(5),
        name="correlations",
    )(*pieces, spectrum, const["into"], const["lags"], reversal(chunk), *deps)


def own_quarter(filter_taps, mirrored, gain):
    taps, width = filter_taps.shape
    cq = width // INNER

    def kernel(taps_ref, mirror_ref, gain_ref, flip, taps_out, mirror_out, gain_out):
        at = columns(group_index(), cq)
        taps_out[...] = taps_ref[:, at]
        gain_out[...] = gain_ref[:, at]
        mirror_out[...] = dot(mirror_ref[...], flip[...]).astype(BF16)

    return pl.pallas_call(
        kernel,
        out_shape=[shape((taps, cq), BF16), shape((taps, cq), BF16), shape((1, cq), F32)],
        in_specs=[VMEM] * 4,
        out_specs=[VMEM] * 3,
        compiler_params=params(16),
        cost_estimate=cost(1),
        name="own_quarter",
    )(filter_taps, mirrored, gain, reversal(cq))


def project(conv, choices, dtype, deps=()):
    span, cq = conv[0].shape
    o_rows, width = choices[0][1].shape
    tile = span // INNER

    def kernel(*refs):
        blocks = refs[INNER : INNER + len(choices)]
        out, token, rhs, sem = refs[INNER + len(choices) + len(deps) :]
        q = group_index()
        z = lax.div(lax.axis_index("seq"), INNER)
        early = lax.axis_index("ch") == lax.div(z, 2)
        end = (z == 0) | (z == 3)
        late, inside = jnp.logical_not(early), jnp.logical_not(end)
        holds = {
            "early": early,
            "late": late,
            "early_end": early & end,
            "early_mid": early & inside,
            "late_end": late & end,
            "late_mid": late & inside,
        }
        for (condition, _), block in zip(choices, blocks):
            @pl.when(holds[condition])
            def _():
                copy = pltpu.make_async_copy(block, rhs, sem)
                copy.start()
                copy.wait()

        token[...] = jnp.zeros(TOKEN, F32)
        for t in range(INNER):
            at = slice(t * tile, (t + 1) * tile)
            total = 0.0
            for k in range(INNER):
                total += dot_nt(refs[k][at, :], rhs[:, columns(q ^ k, cq)])
            out[at, :] = total.astype(dtype)

    return pl.pallas_call(
        kernel,
        out_shape=[shape((span, o_rows), dtype), shape(TOKEN, F32)],
        in_specs=[VMEM] * INNER + [HBM] * len(choices) + [ANY] * len(deps),
        out_specs=[VMEM] * 2,
        scratch_shapes=[pltpu.VMEM((o_rows, width), BF16), pltpu.SemaphoreType.DMA],
        compiler_params=params(16),
        cost_estimate=cost(3),
        name="project",
    )(*conv, *[block for _, block in choices], *deps)


def summed_rows(kept, received, dtype, deps=()):
    n = len(received)
    span, width = kept.shape
    rows = span // INNER

    def kernel(kept_ref, *rest):
        q, outs = group_index(), rest[n + len(deps) :]
        for k in range(INNER):
            at = pl.ds(pl.multiple_of((q ^ k) * rows, rows), rows)
            total = kept_ref[at, :]
            for got_ref in rest[:n]:
                total += got_ref[at, :].astype(F32)
            outs[k][...] = total.astype(dtype)

    return pl.pallas_call(
        kernel,
        out_shape=[shape((rows, width), dtype)] * INNER,
        in_specs=[VMEM] * (1 + n) + [ANY] * len(deps),
        out_specs=[VMEM] * INNER,
        compiler_params=params(16),
        cost_estimate=cost(1),
        name="summed_rows",
    )(kept, *received, *deps)


def assembled(first, second, width):
    rows, o_rows = first[0].shape

    def kernel(*refs):
        q = group_index()
        z = lax.div(lax.axis_index("seq"), INNER)
        for r in range(2):
            for k in range(INNER):
                block = (lax.rem(z, 2) ^ r) * INNER + (q ^ k)
                refs[-1][:, columns(block, o_rows)] = refs[r * INNER + k][...]

    return pl.pallas_call(
        kernel,
        out_shape=shape((rows, width), BF16),
        in_specs=[VMEM] * (2 * INNER),
        out_specs=VMEM,
        compiler_params=params(16),
        cost_estimate=cost(1),
        name="assembled",
    )(*first, *second)


def lag_blocks(forward, mirrored, count, deps):
    taps, cq = forward.shape
    lags = taps // count

    def kernel(forward_ref, mirrored_ref, *rest):
        z = lax.div(lax.axis_index("seq"), INNER)
        for k, out in enumerate(rest[len(deps) :]):
            at = pl.ds(pl.multiple_of((z ^ k) * lags, lags), lags)
            out[...] = (forward_ref[at, :] + mirrored_ref[at, :].astype(F32)).astype(out.dtype)

    return pl.pallas_call(
        kernel,
        out_shape=[shape((lags, cq), F32)] + [shape((lags, cq), BF16)] * (count - 1),
        in_specs=[VMEM] * 2 + [ANY] * len(deps),
        out_specs=[VMEM] * count,
        compiler_params=params(8),
        cost_estimate=cost(1),
        name="lag_blocks",
    )(forward, mirrored, *deps)


def side_by_side(pieces):
    rows, cq = pieces[0].shape

    def kernel(*refs):
        q = group_index()
        for k in range(INNER):
            refs[INNER][:, columns(q ^ k, cq)] = refs[k][...]
        refs[-1][...] = jnp.zeros(TOKEN, F32)

    return pl.pallas_call(
        kernel,
        out_shape=[shape((rows, INNER * cq), pieces[0].dtype), shape(TOKEN, F32)],
        in_specs=[VMEM] * INNER,
        out_specs=[VMEM] * 2,
        compiler_params=params(8),
        cost_estimate=cost(1),
        name="side_by_side",
    )(*pieces)


def placed_by_source(pieces, q):
    result = jnp.zeros((INNER,) + pieces[0].shape, pieces[0].dtype)
    for k, piece in enumerate(pieces):
        result = lax.dynamic_update_index_in_dim(result, piece, q ^ k, 0)
    return result


def by_member(value, q):
    return [lax.dynamic_index_in_dim(value, q ^ k, 0, keepdims=False) for k in range(INNER)]


def pick_member(pieces, q, member):
    result = pieces[0]
    for k in range(1, INNER):
        result = jnp.where((q ^ k) == member, pieces[k], result)
    return result


def body(grad_out, saved_in, filter_taps, skip_gain, projection):
    rows, width = grad_out.shape
    taps = filter_taps.shape[0]
    n_seq, n_ch = lax.axis_size("seq"), lax.axis_size("ch")
    outer = n_seq // INNER
    cq = width // INNER
    span = INNER * rows
    window = span + 2 * rows
    seq = lax.axis_index("seq")
    q, z = seq % INNER, seq // INNER
    const = transforms(rows)
    special = outer == 4 and n_ch == 2

    if special:
        shift = lambda v, table: lax.ppermute(
            v, "seq", [(INNER * a + i, INNER * b + i) for a, b in table for i in range(INNER)]
        )
        near = shift(projection, [(0, 1), (1, 0), (2, 3), (3, 2)])
        mid = shift(projection, [(1, 2), (2, 1)])

    singles = [(k,) for k in range(INNER)]
    grads = spread(quarters(grad_out, singles))
    mirrored = mirror_ch(quarters(filter_taps, [(0,)], reverse=True)[0])
    quarter = own_quarter(filter_taps, mirrored, skip_gain.reshape(1, width))

    final, initial = pick_member(grads, q, INNER - 1), pick_member(grads, q, 0)
    before = lax.ppermute(final, "seq", [(i, i + INNER) for i in range(n_seq - INNER)])
    after = lax.ppermute(initial, "seq", [(i + INNER, i) for i in range(n_seq - INNER)])
    near_ones = ()
    if special:
        near_ones = (near, mid)
        far_ends = shift(mid, [(1, 0), (2, 3)])
        far_mid = shift(near, [(2, 1), (1, 2)])
        last = shift(far_mid, [(1, 0), (2, 3)])
    input_own, input_near, input_far = quarters(saved_in, [(0,), (1,), (2, 3)], (grads[2],))
    input_far = swap_seq(input_far, 2)
    inputs = [input_own, swap_seq(input_near, 1), input_far[0], swap_seq(input_far[1], 1)]
    spectrum, conv = filtered(grads, before, after, *quarter, const, (input_far,), near_ones)

    conv2 = swap_seq(conv, 2)
    conv1 = swap_seq(conv, 1)
    scale = 2.0 / window / math.sqrt(rows * n_seq)
    forward, turned, token = correlations(inputs, spectrum, const, scale, ())
    conv3 = swap_seq(tie(conv2, token), 1)
    conv_parts = [conv, conv1, conv2, conv3]

    mirrored = lax.ppermute(
        turned,
        ("seq", "ch"),
        [
            (s * n_ch + c, (s ^ (INNER - 1)) * n_ch + n_ch - 1 - c)
            for s in range(n_seq)
            for c in range(n_ch)
        ],
    )
    if special:
        x2 = [("end", far_ends), ("mid", far_mid)]
        x3 = [("end", last), ("mid", mid)]
        sent = lambda late, soon: [("early_" + w, block) for w, block in late] + [("late", soon)]
        kept = lambda late, soon: [("late_" + w, block) for w, block in late] + [("early", soon)]
        first, token = project(conv_parts, sent(x2, projection), BF16, (token,))
        got = mirror_ch(first)
        own, token = project(conv_parts, kept(x2, projection), F32, (token,))
        second, token = project(conv_parts, sent(x3, near), BF16, (token,))
        got2 = mirror_ch(second)
        lag_own, *lag_sent = lag_blocks(forward, mirrored, outer, (token,))
        lag_got = [swap_seq(block, INNER * (k + 1)) for k, block in enumerate(lag_sent)]
        moved = spread(summed_rows(own, [got], BF16, (token,)))
        own2, token = project(conv_parts, kept(x3, near), F32, (token,))
        lag_pieces = summed_rows(lag_own, lag_got, F32)
        filter_grad, filter_token = side_by_side(spread(lag_pieces))
        moved2 = spread(summed_rows(own2, [got2], BF16, tuple(moved)))
        grad_in = assembled(moved, moved2, width)
    else:
        groups = [[INNER * a + i for a in range(outer)] for i in range(INNER)]
        proj_all = lax.all_gather(projection, "seq", axis=0, axis_index_groups=groups)
        conv_all = placed_by_source(conv_parts, q)
        partial_value = lax.dot_general(
            conv_all.transpose(1, 0, 2).reshape(span, width),
            proj_all.reshape(-1, width),
            (((1,), (1,)), ((), ())),
            preferred_element_type=F32,
        )
        total = lax.psum_scatter(
            partial_value.astype(BF16), "ch", scatter_dimension=1, tiled=True
        )
        o_rows = projection.shape[0]
        moved = spread(by_member(total.reshape(INNER, rows, -1), q))
        stacked = placed_by_source(moved, q).reshape(INNER, rows, -1, o_rows)
        grad_in = stacked.transpose(1, 2, 0, 3).reshape(rows, width)

        summed = lax.psum_scatter(
            forward + mirrored.astype(F32), "seq", scatter_dimension=0, tiled=True, axis_index_groups=groups
        )
        lag_pieces = by_member(summed.reshape(INNER, -1, cq), q)
        filter_grad, _ = side_by_side(spread(lag_pieces))
    return (grad_in, filter_grad)


def solution(mesh):
    placed = (P("seq", "ch"), P("seq", "ch"), P(None, "ch"), P("ch"), P("seq", "ch"))
    return jax.shard_map(
        body,
        mesh=mesh,
        in_specs=placed,
        out_specs=(P("seq", "ch"), P("seq", "ch")),
        check_vma=False,
    )
```

```python
import math

import jax
import jax.numpy as jnp
import numpy as np
from jax import lax
from jax.experimental import pallas as pl
from jax.experimental.pallas import tpu as pltpu
from jax.sharding import PartitionSpec as P

INNER = 4
F32, BF16 = jnp.float32, jnp.bfloat16
VMEM = pl.BlockSpec(memory_space=pltpu.VMEM)
ANY = pl.BlockSpec(memory_space=pl.ANY)
HBM = pl.BlockSpec(memory_space=pltpu.HBM)
TOKEN = (8, 128)
MIB = 1 << 20
SMALL = pl.CostEstimate(flops=1000, bytes_accessed=1000, transcendentals=0)


def cost(us):
    return pl.CostEstimate(flops=int(us * 1e9), bytes_accessed=int(us * 1e6), transcendentals=0)


def params(mib):
    return pltpu.CompilerParams(vmem_limit_bytes=mib * MIB)


def shape(dims, dtype):
    return jax.ShapeDtypeStruct(dims, dtype)


def swap_seq(value, k):
    count = lax.axis_size("seq")
    return lax.ppermute(value, "seq", [(i, i ^ k) for i in range(count)])


def mirror_ch(value):
    count = lax.axis_size("ch")
    return lax.ppermute(value, "ch", [(i, count - 1 - i) for i in range(count)])


def group_index():
    return lax.rem(lax.axis_index("seq"), INNER)


def columns(block, width):
    return pl.ds(pl.multiple_of(block * width, width), width)


def dot(a, b):
    return jnp.dot(a, b, preferred_element_type=F32)


def dot_nt(a, b):
    return lax.dot_general(a, b, (((1,), (1,)), ((), ())), preferred_element_type=F32)


BLOCKS = INNER + 2
PAIRS = BLOCKS // 2


def angles(j):
    return [2 * math.pi * (j + 0.5) * b / BLOCKS for b in range(BLOCKS)]


def exact(value):
    return 0.0 if abs(value) < 1e-9 else float(value)


def transforms(rows):
    window = BLOCKS * rows
    into, at_taps = [], []
    for j in range(PAIRS):
        upper, lower = [], []
        for index, sign in ((j, 1.0), (BLOCKS - 1 - j, -1.0)):
            k = np.arange(index, window // 2, BLOCKS)
            angle = 2 * np.pi * (k + 0.5)[:, None] * np.arange(rows)[None, :] / window
            c, s = np.cos(angle), np.sin(angle)
            upper += [np.concatenate([c, sign * s], 1), np.concatenate([-s, sign * c], 1)]
            lower += [c, s]
        into.append(np.concatenate(upper, 0))
        at_taps.append(np.concatenate(lower, 0))
    into, at_taps = np.stack(into), np.stack(at_taps)
    cast = lambda a: np.ascontiguousarray(a).astype(np.float32).astype(BF16)
    turn = lambda a: a.transpose(0, 2, 1)
    return {
        "into": cast(into),
        "back": cast(turn(into)),
        "taps": cast(at_taps),
        "lags": cast(turn(at_taps)),
    }


def reversal(count):
    return np.eye(count, dtype=np.float32)[::-1].astype(BF16)


def halves_after(value, *deps):
    half = value.shape[0] // 2

    def kernel(value_ref, *rest):
        rest[-2][...] = value_ref[:half]
        rest[-1][...] = value_ref[half:]

    return pl.pallas_call(
        kernel,
        out_shape=[shape((half, value.shape[1]), value.dtype)] * 2,
        in_specs=[VMEM] + [ANY] * len(deps),
        out_specs=[VMEM] * 2,
        compiler_params=params(8),
        cost_estimate=SMALL,
        name="halves_after",
    )(value, *deps)


def quarters(value, outputs, deps=(), reverse=False):
    rows, width = value.shape
    cq = width // INNER
    total = sum(len(members) for members in outputs)

    def kernel(*refs):
        q = group_index()
        if reverse:
            q = INNER - 1 - q
        outs, sems = refs[1 + len(deps) : -1], refs[-1]
        copies = []
        for members, out in zip(outputs, outs):
            for i, k in enumerate(members):
                source = refs[0].at[:, columns(q ^ k, cq)]
                target = out if len(members) == 1 else out.at[i]
                copies.append(pltpu.make_async_copy(source, target, sems.at[len(copies)]))
        for copy in copies:
            copy.start()
        for copy in copies:
            copy.wait()

    dims = [(rows, cq) if len(m) == 1 else (len(m), rows, cq) for m in outputs]
    return pl.pallas_call(
        kernel,
        out_shape=[shape(d, value.dtype) for d in dims],
        in_specs=[HBM] + [ANY] * len(deps),
        out_specs=[ANY] * len(outputs),
        scratch_shapes=[pltpu.SemaphoreType.DMA((total,))],
        compiler_params=params(8),
        cost_estimate=cost(1),
        name="quarters",
    )(value, *deps)


def spread(pieces):
    return [pieces[0]] + [swap_seq(pieces[k], k) for k in range(1, INNER)]


def combined(blocks, first, j):
    re, im = 0.0, 0.0
    for i, block in enumerate(blocks):
        angle = angles(j)[first + i]
        c, s = exact(math.cos(angle)), exact(-math.sin(angle))
        if c:
            re = re + c * block
        if s:
            im = im + s * block
    return jnp.concatenate([re.astype(BF16), im.astype(BF16)], 0)


def complex_rows(value, n):
    return [(value[2 * i * n : (2 * i + 1) * n], value[(2 * i + 1) * n : (2 * i + 2) * n]) for i in range(2)]


def chunk_of(cq):
    return min(256, cq)


def filtered(pieces, before, after, own_taps, mirrored, gain, const, deps, large):
    rows, cq = pieces[0].shape
    taps = own_taps.shape[0]
    chunk = chunk_of(cq)
    n = rows // 2
    scale = 2.0 / (BLOCKS * rows)

    def kernel(*refs):
        before_ref, after_ref, taps_ref, mirror_ref, gain_ref, into, back, at_taps = refs[INNER : INNER + 8]
        spectrum, conv, ordered = refs[INNER + 8 + len(deps) + len(large) :]
        q = group_index()
        for k in range(INNER):
            ordered[q ^ k] = refs[k][...].astype(F32)
        blocks = [before_ref[...].astype(F32)] + [ordered[i] for i in range(INNER)] + [after_ref[...].astype(F32)]
        direct = gain_ref[...]
        outs = [0.0] * INNER
        for j in range(PAIRS):
            g = dot(into[j], combined(blocks, 0, j))
            spectrum[j] = g.astype(BF16)
            own, other = dot(at_taps[j], taps_ref[...]), dot(at_taps[j], mirror_ref[...])
            product = []
            for (gr, gi), (ar, ai), (br, bi) in zip(
                complex_rows(g, n), complex_rows(own, n), complex_rows(other, n)
            ):
                hr, hi = (ar + br + direct) * scale, (ai - bi) * scale
                product += [(gr * hr - gi * hi).astype(BF16), (gr * hi + gi * hr).astype(BF16)]
            w = dot(back[j], jnp.concatenate(product, 0))
            for i in range(INNER):
                angle = angles(j)[i + 1]
                c, s = exact(math.cos(angle)), exact(-math.sin(angle))
                if c:
                    outs[i] = outs[i] + c * w[:rows]
                if s:
                    outs[i] = outs[i] + s * w[rows:]
        for i in range(INNER):
            conv[i * rows : (i + 1) * rows, :] = outs[i].astype(BF16)

    cols = lambda r: pl.BlockSpec((r, chunk), lambda i: (0, i))
    whole = lambda a: pl.BlockSpec(a.shape, lambda i: (0, 0, 0))
    return pl.pallas_call(
        kernel,
        grid=(cq // chunk,),
        out_shape=[shape((PAIRS, 2 * rows, cq), BF16), shape((INNER * rows, cq), BF16)],
        in_specs=[cols(rows)] * (INNER + 2)
        + [cols(taps)] * 2
        + [cols(1)]
        + [whole(const["into"]), whole(const["back"]), whole(const["taps"])]
        + [ANY] * len(deps)
        + [HBM] * len(large),
        out_specs=[pl.BlockSpec((PAIRS, 2 * rows, chunk), lambda i: (0, 0, i)), cols(INNER * rows)],
        scratch_shapes=[pltpu.VMEM((INNER, rows, chunk), F32)],
        compiler_params=params(32),
        cost_estimate=cost(6),
        name="filtered",
    )(*pieces, before, after, own_taps, mirrored, gain, const["into"], const["back"], const["taps"], *deps, *large)


def correlations(pieces, spectrum, const, scale, deps):
    rows, cq = pieces[0].shape
    taps = const["lags"].shape[1]
    chunk = chunk_of(cq)
    n = rows // 2
    chunks = cq // chunk

    def kernel(*refs):
        spec, into, lags, flip = refs[INNER : INNER + 4]
        forward, turned, token, ordered = refs[INNER + 4 + len(deps) :]
        token[...] = jnp.zeros(TOKEN, F32)
        q = group_index()
        for k in range(INNER):
            ordered[q ^ k] = refs[k][...].astype(F32)
        blocks = [ordered[i] for i in range(INNER)]
        even, odd = 0.0, 0.0
        for j in range(PAIRS):
            x = dot(into[j], combined(blocks, 1, j))
            g = spec[j].astype(F32)
            for i, ((xr, xi), (gr, gi)) in enumerate(zip(complex_rows(x, n), complex_rows(g, n))):
                z_re = ((gr * xr + gi * xi) * scale).astype(BF16)
                z_im = ((gi * xr - gr * xi) * scale).astype(BF16)
                even += dot(lags[j, :, 2 * i * n : (2 * i + 1) * n], z_re)
                odd += dot(lags[j, :, (2 * i + 1) * n : (2 * i + 2) * n], z_im)
        forward[...] = even - odd
        turned[...] = dot((even + odd).astype(BF16), flip[...]).astype(BF16)

    cols = lambda r: pl.BlockSpec((r, chunk), lambda i: (0, i))
    whole = lambda a: pl.BlockSpec(a.shape, lambda i: (0, 0, 0))
    return pl.pallas_call(
        kernel,
        grid=(chunks,),
        out_shape=[shape((taps, cq), F32), shape((taps, cq), BF16), shape(TOKEN, F32)],
        in_specs=[cols(rows)] * INNER
        + [pl.BlockSpec((PAIRS, 2 * rows, chunk), lambda i: (0, 0, i))]
        + [whole(const["into"]), whole(const["lags"]), pl.BlockSpec((chunk, chunk), lambda i: (0, 0))]
        + [HBM] * len(deps),
        out_specs=[
            cols(taps),
            pl.BlockSpec((taps, chunk), lambda i: (0, chunks - 1 - i)),
            pl.BlockSpec(TOKEN, lambda i: (0, 0)),
        ],
        scratch_shapes=[pltpu.VMEM((INNER, rows, chunk), F32)],
        compiler_params=params(32),
        cost_estimate=cost(0.1),
        name="correlations",
    )(*pieces, spectrum, const["into"], const["lags"], reversal(chunk), *deps)


def own_quarter(filter_taps, mirrored, gain):
    taps, width = filter_taps.shape
    cq = width // INNER

    def kernel(taps_ref, mirror_ref, gain_ref, flip, taps_out, mirror_out, gain_out):
        at = columns(group_index(), cq)
        taps_out[...] = taps_ref[:, at]
        gain_out[...] = gain_ref[:, at]
        mirror_out[...] = dot(mirror_ref[...], flip[...]).astype(BF16)

    return pl.pallas_call(
        kernel,
        out_shape=[shape((taps, cq), BF16), shape((taps, cq), BF16), shape((1, cq), F32)],
        in_specs=[VMEM] * 4,
        out_specs=[VMEM] * 3,
        compiler_params=params(16),
        cost_estimate=cost(1),
        name="own_quarter",
    )(filter_taps, mirrored, gain, reversal(cq))


def project(conv, choices, dtype, deps=()):
    span, cq = conv[0].shape
    o_rows, width = choices[0][1].shape
    tile = span // INNER

    def kernel(*refs):
        blocks = refs[INNER + 1 : INNER + 1 + len(choices)]
        out, token, rhs, sem = refs[INNER + 1 + len(choices) + len(deps) :]
        q = group_index()
        z = lax.div(lax.axis_index("seq"), INNER)
        early = lax.axis_index("ch") == lax.div(z, 2)
        end = (z == 0) | (z == 3)
        late, inside = jnp.logical_not(early), jnp.logical_not(end)
        holds = {
            "early": early,
            "late": late,
            "early_end": early & end,
            "early_mid": early & inside,
            "late_end": late & end,
            "late_mid": late & inside,
        }
        for (condition, _), block in zip(choices, blocks):
            @pl.when(holds[condition])
            def _():
                copy = pltpu.make_async_copy(block, rhs, sem)
                copy.start()
                copy.wait()

        token[...] = jnp.zeros(TOKEN, F32)
        for t in range(INNER):
            at = slice(t * tile, (t + 1) * tile)
            total = 0.0
            for k in range(INNER - 1):
                total += dot_nt(refs[k][at, :], rhs[:, columns(q ^ k, cq)])
            within = slice(t % 2 * tile, (t % 2 + 1) * tile)
            total += dot_nt(refs[INNER - 1 + t // 2][within, :], rhs[:, columns(q ^ (INNER - 1), cq)])
            out[at, :] = total.astype(dtype)

    return pl.pallas_call(
        kernel,
        out_shape=[shape((span, o_rows), dtype), shape(TOKEN, F32)],
        in_specs=[VMEM] * (INNER + 1) + [HBM] * len(choices) + [ANY] * len(deps),
        out_specs=[VMEM] * 2,
        scratch_shapes=[pltpu.VMEM((o_rows, width), BF16), pltpu.SemaphoreType.DMA],
        compiler_params=params(16),
        cost_estimate=SMALL,
        name="project",
    )(*conv, *[block for _, block in choices], *deps)


def summed_rows(kept, got, lags, deps=()):
    span, width = kept.shape
    rows = span // INNER
    count = len(lags)
    lag_rows = lags[0].shape[0] // INNER if lags else 0
    folds = lags[0].shape[1] // width if lags else 0

    def kernel(kept_ref, got_ref, *rest):
        q = group_index()
        for k, out in enumerate(rest[count + len(deps) :]):
            at = pl.ds(pl.multiple_of((q ^ k) * rows, rows), rows)
            out[:rows, :] = (kept_ref[at, :] + got_ref[at, :].astype(F32)).astype(BF16)
            if lags:
                at = pl.ds(pl.multiple_of((q ^ k) * lag_rows, lag_rows), lag_rows)
                total = 0.0
                for lag_ref in rest[:count]:
                    total += lag_ref[at, :].astype(F32)
                for fold in range(folds):
                    to = rows + fold * lag_rows
                    out[to : to + lag_rows, :] = total[:, fold * width : (fold + 1) * width].astype(BF16)

    return pl.pallas_call(
        kernel,
        out_shape=[shape((rows + folds * lag_rows, width), BF16)] * INNER,
        in_specs=[VMEM] * (2 + count) + [ANY] * len(deps),
        out_specs=[VMEM] * INNER,
        compiler_params=params(16),
        cost_estimate=cost(1),
        name="summed_rows",
    )(kept, got, *lags, *deps)


def assembled(first, second, width):
    rows, o_rows = first[0].shape
    folds = width // INNER // o_rows
    lag_rows = (second[0].shape[0] - rows) // folds

    def kernel(*refs):
        q = group_index()
        z = lax.div(lax.axis_index("seq"), INNER)
        out, filter_out = refs[-2:]
        for r in range(2):
            for k in range(INNER):
                block = (lax.rem(z, 2) ^ r) * INNER + (q ^ k)
                out[:, columns(block, o_rows)] = refs[r * INNER + k][:rows, :]
        for k in range(INNER):
            for fold in range(folds):
                at = rows + fold * lag_rows
                lag = refs[INNER + k][at : at + lag_rows, :]
                filter_out[:, columns((q ^ k) * folds + fold, o_rows)] = lag.astype(F32)

    return pl.pallas_call(
        kernel,
        out_shape=[shape((rows, width), BF16), shape((lag_rows, width), F32)],
        in_specs=[VMEM] * (2 * INNER),
        out_specs=[VMEM] * 2,
        compiler_params=params(16),
        cost_estimate=cost(1),
        name="assembled",
    )(*first, *second)


def lag_blocks(forward, mirrored, count, deps):
    taps, cq = forward.shape
    lags = taps // count

    def kernel(forward_ref, mirrored_ref, *rest):
        z = lax.div(lax.axis_index("seq"), INNER)
        for k, out in enumerate(rest[len(deps) :]):
            at = pl.ds(pl.multiple_of((z ^ k) * lags, lags), lags)
            out[...] = (forward_ref[at, :] + mirrored_ref[at, :].astype(F32)).astype(out.dtype)

    return pl.pallas_call(
        kernel,
        out_shape=[shape((lags, cq), F32)] + [shape((lags, cq), BF16)] * (count - 1),
        in_specs=[VMEM] * 2 + [ANY] * len(deps),
        out_specs=[VMEM] * count,
        compiler_params=params(8),
        cost_estimate=cost(1),
        name="lag_blocks",
    )(forward, mirrored, *deps)


def side_by_side(pieces):
    rows, cq = pieces[0].shape

    def kernel(*refs):
        q = group_index()
        for k in range(INNER):
            refs[INNER][:, columns(q ^ k, cq)] = refs[k][...]
        refs[-1][...] = jnp.zeros(TOKEN, F32)

    return pl.pallas_call(
        kernel,
        out_shape=[shape((rows, INNER * cq), pieces[0].dtype), shape(TOKEN, F32)],
        in_specs=[VMEM] * INNER,
        out_specs=[VMEM] * 2,
        compiler_params=params(8),
        cost_estimate=cost(1),
        name="side_by_side",
    )(*pieces)


def placed_by_source(pieces, q):
    result = jnp.zeros((INNER,) + pieces[0].shape, pieces[0].dtype)
    for k, piece in enumerate(pieces):
        result = lax.dynamic_update_index_in_dim(result, piece, q ^ k, 0)
    return result


def by_member(value, q):
    return [lax.dynamic_index_in_dim(value, q ^ k, 0, keepdims=False) for k in range(INNER)]


def pick_member(pieces, q, member):
    result = pieces[0]
    for k in range(1, INNER):
        result = jnp.where((q ^ k) == member, pieces[k], result)
    return result


def body(grad_out, saved_in, filter_taps, skip_gain, projection):
    rows, width = grad_out.shape
    taps = filter_taps.shape[0]
    n_seq, n_ch = lax.axis_size("seq"), lax.axis_size("ch")
    outer = n_seq // INNER
    cq = width // INNER
    span = INNER * rows
    window = span + 2 * rows
    seq = lax.axis_index("seq")
    q, z = seq % INNER, seq // INNER
    const = transforms(rows)
    special = outer == 4 and n_ch == 2

    if special:
        shift = lambda v, table: lax.ppermute(
            v, "seq", [(INNER * a + i, INNER * b + i) for a, b in table for i in range(INNER)]
        )
        near = shift(projection, [(0, 1), (1, 0), (2, 3), (3, 2)])
        mid = shift(projection, [(1, 2), (2, 1)])

    singles = [(k,) for k in range(INNER)]
    grads = spread(quarters(grad_out, singles))
    mirrored = mirror_ch(quarters(filter_taps, [(0,)], reverse=True)[0])
    quarter = own_quarter(filter_taps, mirrored, skip_gain.reshape(1, width))

    final, initial = pick_member(grads, q, INNER - 1), pick_member(grads, q, 0)
    before = lax.ppermute(final, "seq", [(i, i + INNER) for i in range(n_seq - INNER)])
    after = lax.ppermute(initial, "seq", [(i + INNER, i) for i in range(n_seq - INNER)])
    near_ones, far = (), ()
    if special:
        near_ones = (near, mid)
        far_ends = shift(mid, [(1, 0), (2, 3)])
        far_mid = shift(near, [(2, 1), (1, 2)])
        far = (far_mid, far_ends)
        last = shift(far_mid, [(1, 0), (2, 3)])
    input_own, input_near, input_far = quarters(saved_in, [(0,), (1,), (2, 3)], (grads[2],))
    input_far = swap_seq(input_far, 2)
    inputs = [input_own, swap_seq(input_near, 1), input_far[0], swap_seq(input_far[1], 1)]
    spectrum, conv = filtered(grads, before, after, *quarter, const, (input_far,), near_ones)

    conv2 = swap_seq(conv, 2)
    conv1 = swap_seq(conv, 1)
    scale = 2.0 / window / math.sqrt(rows * n_seq)
    forward, turned, token = correlations(inputs, spectrum, const, scale, far)
    conv3 = [swap_seq(half, 1) for half in halves_after(conv2, token)]
    conv_parts = [conv, conv1, conv2, *conv3]

    mirrored = lax.ppermute(
        turned,
        ("seq", "ch"),
        [
            (s * n_ch + c, (s ^ (INNER - 1)) * n_ch + n_ch - 1 - c)
            for s in range(n_seq)
            for c in range(n_ch)
        ],
    )
    if special:
        x2 = [("end", far_ends), ("mid", far_mid)]
        x3 = [("end", last), ("mid", mid)]
        sent = lambda late, soon: [("early_" + w, block) for w, block in late] + [("late", soon)]
        kept = lambda late, soon: [("late_" + w, block) for w, block in late] + [("early", soon)]
        first, token = project(conv_parts, sent(x2, projection), BF16, (token,))
        got = mirror_ch(first)
        own, token = project(conv_parts, kept(x2, projection), F32, (token,))
        lag_own, *lag_sent = lag_blocks(forward, mirrored, outer, ())
        second, token = project(conv_parts, sent(x3, near), BF16, (token, lag_own))
        got2 = mirror_ch(second)
        lag_got = [swap_seq(block, INNER * (k + 1)) for k, block in enumerate(lag_sent)]
        moved = spread(summed_rows(own, got, []))
        own2, token = project(conv_parts, kept(x3, near), F32, (token,))
        moved2 = spread(summed_rows(own2, got2, [lag_own] + lag_got, tuple(moved)))
        grad_in, filter_grad = assembled(moved, moved2, width)
    else:
        groups = [[INNER * a + i for a in range(outer)] for i in range(INNER)]
        proj_all = lax.all_gather(projection, "seq", axis=0, axis_index_groups=groups)
        conv_all = placed_by_source([conv, conv1, conv2, jnp.concatenate(conv3, 0)], q)
        partial_value = lax.dot_general(
            conv_all.transpose(1, 0, 2).reshape(span, width),
            proj_all.reshape(-1, width),
            (((1,), (1,)), ((), ())),
            preferred_element_type=F32,
        )
        total = lax.psum_scatter(
            partial_value.astype(BF16), "ch", scatter_dimension=1, tiled=True
        )
        o_rows = projection.shape[0]
        moved = spread(by_member(total.reshape(INNER, rows, -1), q))
        stacked = placed_by_source(moved, q).reshape(INNER, rows, -1, o_rows)
        grad_in = stacked.transpose(1, 2, 0, 3).reshape(rows, width)

        summed = lax.psum_scatter(
            forward + mirrored.astype(F32), "seq", scatter_dimension=0, tiled=True, axis_index_groups=groups
        )
        lag_pieces = by_member(summed.reshape(INNER, -1, cq), q)
        filter_grad, _ = side_by_side(spread(lag_pieces))
    return (grad_in, filter_grad)


def solution(mesh):
    placed = (P("seq", "ch"), P("seq", "ch"), P(None, "ch"), P("ch"), P("seq", "ch"))
    return jax.shard_map(
        body,
        mesh=mesh,
        in_specs=placed,
        out_specs=(P("seq", "ch"), P("seq", "ch")),
        check_vma=False,
    )
```

```python
import math

import jax
import jax.numpy as jnp
import numpy as np
from jax import lax
from jax.experimental import pallas as pl
from jax.experimental.pallas import tpu as pltpu
from jax.sharding import PartitionSpec as P

INNER = 4
F32, BF16 = jnp.float32, jnp.bfloat16
VMEM = pl.BlockSpec(memory_space=pltpu.VMEM)
ANY = pl.BlockSpec(memory_space=pl.ANY)
HBM = pl.BlockSpec(memory_space=pltpu.HBM)
TOKEN = (8, 128)
MIB = 1 << 20
SMALL = pl.CostEstimate(flops=1000, bytes_accessed=1000, transcendentals=0)


def cost(us):
    return pl.CostEstimate(flops=int(us * 1e9), bytes_accessed=int(us * 1e6), transcendentals=0)


def params(mib):
    return pltpu.CompilerParams(vmem_limit_bytes=mib * MIB)


def shape(dims, dtype):
    return jax.ShapeDtypeStruct(dims, dtype)


def swap_seq(value, k):
    count = lax.axis_size("seq")
    return lax.ppermute(value, "seq", [(i, i ^ k) for i in range(count)])


def mirror_ch(value):
    count = lax.axis_size("ch")
    return lax.ppermute(value, "ch", [(i, count - 1 - i) for i in range(count)])


def group_index():
    return lax.rem(lax.axis_index("seq"), INNER)


def columns(block, width):
    return pl.ds(pl.multiple_of(block * width, width), width)


def dot(a, b):
    return jnp.dot(a, b, preferred_element_type=F32)


def dot_nt(a, b):
    return lax.dot_general(a, b, (((1,), (1,)), ((), ())), preferred_element_type=F32)


BLOCKS = INNER + 2
PAIRS = BLOCKS // 2


def angles(j):
    return [2 * math.pi * (j + 0.5) * b / BLOCKS for b in range(BLOCKS)]


def exact(value):
    return 0.0 if abs(value) < 1e-9 else float(value)


def transforms(rows):
    window = BLOCKS * rows
    into, at_taps = [], []
    for j in range(PAIRS):
        upper, lower = [], []
        for index, sign in ((j, 1.0), (BLOCKS - 1 - j, -1.0)):
            k = np.arange(index, window // 2, BLOCKS)
            angle = 2 * np.pi * (k + 0.5)[:, None] * np.arange(rows)[None, :] / window
            c, s = np.cos(angle), np.sin(angle)
            upper += [np.concatenate([c, sign * s], 1), np.concatenate([-s, sign * c], 1)]
            lower += [c, s]
        into.append(np.concatenate(upper, 0))
        at_taps.append(np.concatenate(lower, 0))
    into, at_taps = np.stack(into), np.stack(at_taps)
    cast = lambda a: np.ascontiguousarray(a).astype(np.float32).astype(BF16)
    turn = lambda a: a.transpose(0, 2, 1)
    return {
        "into": cast(into),
        "back": cast(turn(into)),
        "taps": cast(at_taps),
        "lags": cast(turn(at_taps)),
    }


def reversal(count):
    return np.eye(count, dtype=np.float32)[::-1].astype(BF16)


def halves_after(value, *deps):
    half = value.shape[0] // 2

    def kernel(value_ref, *rest):
        rest[-2][...] = value_ref[:half]
        rest[-1][...] = value_ref[half:]

    return pl.pallas_call(
        kernel,
        out_shape=[shape((half, value.shape[1]), value.dtype)] * 2,
        in_specs=[VMEM] + [ANY] * len(deps),
        out_specs=[VMEM] * 2,
        compiler_params=params(8),
        cost_estimate=SMALL,
        name="halves_after",
    )(value, *deps)


def quarters(value, outputs, deps=(), reverse=False):
    rows, width = value.shape
    cq = width // INNER
    total = sum(len(members) for members in outputs)

    def kernel(*refs):
        q = group_index()
        if reverse:
            q = INNER - 1 - q
        outs, sems = refs[1 + len(deps) : -1], refs[-1]
        copies = []
        for members, out in zip(outputs, outs):
            for i, k in enumerate(members):
                source = refs[0].at[:, columns(q ^ k, cq)]
                target = out if len(members) == 1 else out.at[i]
                copies.append(pltpu.make_async_copy(source, target, sems.at[len(copies)]))
        for copy in copies:
            copy.start()
        for copy in copies:
            copy.wait()

    dims = [(rows, cq) if len(m) == 1 else (len(m), rows, cq) for m in outputs]
    return pl.pallas_call(
        kernel,
        out_shape=[shape(d, value.dtype) for d in dims],
        in_specs=[HBM] + [ANY] * len(deps),
        out_specs=[ANY] * len(outputs),
        scratch_shapes=[pltpu.SemaphoreType.DMA((total,))],
        compiler_params=params(8),
        cost_estimate=cost(1),
        name="quarters",
    )(value, *deps)


def spread(pieces):
    return [pieces[0]] + [swap_seq(pieces[k], k) for k in range(1, INNER)]


def combined(blocks, first, j):
    re, im = 0.0, 0.0
    for i, block in enumerate(blocks):
        angle = angles(j)[first + i]
        c, s = exact(math.cos(angle)), exact(-math.sin(angle))
        if c:
            re = re + c * block
        if s:
            im = im + s * block
    return jnp.concatenate([re.astype(BF16), im.astype(BF16)], 0)


def complex_rows(value, n):
    return [(value[2 * i * n : (2 * i + 1) * n], value[(2 * i + 1) * n : (2 * i + 2) * n]) for i in range(2)]


def chunk_of(cq):
    return min(256, cq)


def filtered(pieces, before, after, own_taps, mirrored, gain, const, deps, large):
    rows, cq = pieces[0].shape
    taps = own_taps.shape[0]
    chunk = chunk_of(cq)
    n = rows // 2
    scale = 2.0 / (BLOCKS * rows)

    def kernel(*refs):
        before_ref, after_ref, taps_ref, mirror_ref, gain_ref, into, back, at_taps = refs[INNER : INNER + 8]
        spectrum, conv, ordered = refs[INNER + 8 + len(deps) + len(large) :]
        q = group_index()
        for k in range(INNER):
            ordered[q ^ k] = refs[k][...].astype(F32)
        blocks = [before_ref[...].astype(F32)] + [ordered[i] for i in range(INNER)] + [after_ref[...].astype(F32)]
        direct = gain_ref[...]
        outs = [0.0] * INNER
        for j in range(PAIRS):
            g = dot(into[j], combined(blocks, 0, j))
            spectrum[j] = g.astype(BF16)
            own, other = dot(at_taps[j], taps_ref[...]), dot(at_taps[j], mirror_ref[...])
            product = []
            for (gr, gi), (ar, ai), (br, bi) in zip(
                complex_rows(g, n), complex_rows(own, n), complex_rows(other, n)
            ):
                hr, hi = (ar + br + direct) * scale, (ai - bi) * scale
                product += [(gr * hr - gi * hi).astype(BF16), (gr * hi + gi * hr).astype(BF16)]
            w = dot(back[j], jnp.concatenate(product, 0))
            for i in range(INNER):
                angle = angles(j)[i + 1]
                c, s = exact(math.cos(angle)), exact(-math.sin(angle))
                if c:
                    outs[i] = outs[i] + c * w[:rows]
                if s:
                    outs[i] = outs[i] + s * w[rows:]
        for i in range(INNER):
            conv[i * rows : (i + 1) * rows, :] = outs[i].astype(BF16)

    cols = lambda r: pl.BlockSpec((r, chunk), lambda i: (0, i))
    whole = lambda a: pl.BlockSpec(a.shape, lambda i: (0, 0, 0))
    return pl.pallas_call(
        kernel,
        grid=(cq // chunk,),
        out_shape=[shape((PAIRS, 2 * rows, cq), BF16), shape((INNER * rows, cq), BF16)],
        in_specs=[cols(rows)] * (INNER + 2)
        + [cols(taps)] * 2
        + [cols(1)]
        + [whole(const["into"]), whole(const["back"]), whole(const["taps"])]
        + [ANY] * len(deps)
        + [HBM] * len(large),
        out_specs=[pl.BlockSpec((PAIRS, 2 * rows, chunk), lambda i: (0, 0, i)), cols(INNER * rows)],
        scratch_shapes=[pltpu.VMEM((INNER, rows, chunk), F32)],
        compiler_params=params(32),
        cost_estimate=cost(6),
        name="filtered",
    )(*pieces, before, after, own_taps, mirrored, gain, const["into"], const["back"], const["taps"], *deps, *large)


def correlations(pieces, spectrum, const, scale, deps):
    rows, cq = pieces[0].shape
    taps = const["lags"].shape[1]
    chunk = chunk_of(cq)
    n = rows // 2
    chunks = cq // chunk

    def kernel(*refs):
        spec, into, lags, flip = refs[INNER : INNER + 4]
        forward, turned, token, ordered = refs[INNER + 4 + len(deps) :]
        token[...] = jnp.zeros(TOKEN, F32)
        q = group_index()
        for k in range(INNER):
            ordered[q ^ k] = refs[k][...].astype(F32)
        blocks = [ordered[i] for i in range(INNER)]
        even, odd = 0.0, 0.0
        for j in range(PAIRS):
            x = dot(into[j], combined(blocks, 1, j))
            g = spec[j].astype(F32)
            for i, ((xr, xi), (gr, gi)) in enumerate(zip(complex_rows(x, n), complex_rows(g, n))):
                z_re = ((gr * xr + gi * xi) * scale).astype(BF16)
                z_im = ((gi * xr - gr * xi) * scale).astype(BF16)
                even += dot(lags[j, :, 2 * i * n : (2 * i + 1) * n], z_re)
                odd += dot(lags[j, :, (2 * i + 1) * n : (2 * i + 2) * n], z_im)
        forward[...] = even - odd
        turned[...] = dot((even + odd).astype(BF16), flip[...]).astype(BF16)

    cols = lambda r: pl.BlockSpec((r, chunk), lambda i: (0, i))
    whole = lambda a: pl.BlockSpec(a.shape, lambda i: (0, 0, 0))
    return pl.pallas_call(
        kernel,
        grid=(chunks,),
        out_shape=[shape((taps, cq), F32), shape((taps, cq), BF16), shape(TOKEN, F32)],
        in_specs=[cols(rows)] * INNER
        + [pl.BlockSpec((PAIRS, 2 * rows, chunk), lambda i: (0, 0, i))]
        + [whole(const["into"]), whole(const["lags"]), pl.BlockSpec((chunk, chunk), lambda i: (0, 0))]
        + [HBM] * len(deps),
        out_specs=[
            cols(taps),
            pl.BlockSpec((taps, chunk), lambda i: (0, chunks - 1 - i)),
            pl.BlockSpec(TOKEN, lambda i: (0, 0)),
        ],
        scratch_shapes=[pltpu.VMEM((INNER, rows, chunk), F32)],
        compiler_params=params(32),
        cost_estimate=cost(0.1),
        name="correlations",
    )(*pieces, spectrum, const["into"], const["lags"], reversal(chunk), *deps)


def own_quarter(filter_taps, mirrored, gain):
    taps, width = filter_taps.shape
    cq = width // INNER

    def kernel(taps_ref, mirror_ref, gain_ref, flip, taps_out, mirror_out, gain_out):
        at = columns(group_index(), cq)
        taps_out[...] = taps_ref[:, at]
        gain_out[...] = gain_ref[:, at]
        mirror_out[...] = dot(mirror_ref[...], flip[...]).astype(BF16)

    return pl.pallas_call(
        kernel,
        out_shape=[shape((taps, cq), BF16), shape((taps, cq), BF16), shape((1, cq), F32)],
        in_specs=[VMEM] * 4,
        out_specs=[VMEM] * 3,
        compiler_params=params(16),
        cost_estimate=cost(1),
        name="own_quarter",
    )(filter_taps, mirrored, gain, reversal(cq))


def project(conv, choices, dtype, deps=()):
    span, cq = conv[0].shape
    o_rows, width = choices[0][1].shape
    tile = span // INNER

    def kernel(*refs):
        blocks = refs[INNER + 1 : INNER + 1 + len(choices)]
        out, token, rhs, sem = refs[INNER + 1 + len(choices) + len(deps) :]
        q = group_index()
        z = lax.div(lax.axis_index("seq"), INNER)
        early = lax.axis_index("ch") == lax.div(z, 2)
        end = (z == 0) | (z == 3)
        late, inside = jnp.logical_not(early), jnp.logical_not(end)
        holds = {
            "early": early,
            "late": late,
            "early_end": early & end,
            "early_mid": early & inside,
            "late_end": late & end,
            "late_mid": late & inside,
        }
        for (condition, _), block in zip(choices, blocks):
            @pl.when(holds[condition])
            def _():
                copy = pltpu.make_async_copy(block, rhs, sem)
                copy.start()
                copy.wait()

        token[...] = jnp.zeros(TOKEN, F32)
        for t in range(INNER):
            at = slice(t * tile, (t + 1) * tile)
            total = 0.0
            for k in range(INNER - 1):
                total += dot_nt(refs[k][at, :], rhs[:, columns(q ^ k, cq)])
            within = slice(t % 2 * tile, (t % 2 + 1) * tile)
            total += dot_nt(refs[INNER - 1 + t // 2][within, :], rhs[:, columns(q ^ (INNER - 1), cq)])
            out[at, :] = total.astype(dtype)

    return pl.pallas_call(
        kernel,
        out_shape=[shape((span, o_rows), dtype), shape(TOKEN, F32)],
        in_specs=[VMEM] * (INNER + 1) + [HBM] * len(choices) + [ANY] * len(deps),
        out_specs=[VMEM] * 2,
        scratch_shapes=[pltpu.VMEM((o_rows, width), BF16), pltpu.SemaphoreType.DMA],
        compiler_params=params(16),
        cost_estimate=SMALL,
        name="project",
    )(*conv, *[block for _, block in choices], *deps)


def summed_rows(kept, got, lags, deps=()):
    span, width = kept.shape
    rows = span // INNER
    count = len(lags)
    lag_rows = lags[0].shape[0] // INNER if lags else 0
    folds = lags[0].shape[1] // width if lags else 0

    def kernel(kept_ref, got_ref, *rest):
        q = group_index()
        for k, out in enumerate(rest[count + len(deps) :]):
            at = pl.ds(pl.multiple_of((q ^ k) * rows, rows), rows)
            out[:rows, :] = (kept_ref[at, :] + got_ref[at, :].astype(F32)).astype(BF16)
            if lags:
                at = pl.ds(pl.multiple_of((q ^ k) * lag_rows, lag_rows), lag_rows)
                total = 0.0
                for lag_ref in rest[:count]:
                    total += lag_ref[at, :].astype(F32)
                for fold in range(folds):
                    to = rows + fold * lag_rows
                    out[to : to + lag_rows, :] = total[:, fold * width : (fold + 1) * width].astype(BF16)

    return pl.pallas_call(
        kernel,
        out_shape=[shape((rows + folds * lag_rows, width), BF16)] * INNER,
        in_specs=[VMEM] * (2 + count) + [ANY] * len(deps),
        out_specs=[VMEM] * INNER,
        compiler_params=params(16),
        cost_estimate=cost(1),
        name="summed_rows",
    )(kept, got, *lags, *deps)


def assembled(first, second, width):
    rows, o_rows = first[0].shape
    folds = width // INNER // o_rows
    lag_rows = (second[0].shape[0] - rows) // folds

    def kernel(*refs):
        q = group_index()
        z = lax.div(lax.axis_index("seq"), INNER)
        out, filter_out = refs[-2:]
        for r in range(2):
            for k in range(INNER):
                block = (lax.rem(z, 2) ^ r) * INNER + (q ^ k)
                out[:, columns(block, o_rows)] = refs[r * INNER + k][:rows, :]
        for k in range(INNER):
            for fold in range(folds):
                at = rows + fold * lag_rows
                lag = refs[INNER + k][at : at + lag_rows, :]
                filter_out[:, columns((q ^ k) * folds + fold, o_rows)] = lag.astype(F32)

    return pl.pallas_call(
        kernel,
        out_shape=[shape((rows, width), BF16), shape((lag_rows, width), F32)],
        in_specs=[VMEM] * (2 * INNER),
        out_specs=[VMEM] * 2,
        compiler_params=params(16),
        cost_estimate=cost(1),
        name="assembled",
    )(*first, *second)


def lag_blocks(forward, mirrored, count, deps):
    taps, cq = forward.shape
    lags = taps // count

    def kernel(forward_ref, mirrored_ref, *rest):
        z = lax.div(lax.axis_index("seq"), INNER)
        for k, out in enumerate(rest[len(deps) :]):
            at = pl.ds(pl.multiple_of((z ^ k) * lags, lags), lags)
            out[...] = (forward_ref[at, :] + mirrored_ref[at, :].astype(F32)).astype(out.dtype)

    return pl.pallas_call(
        kernel,
        out_shape=[shape((lags, cq), F32)] + [shape((lags, cq), BF16)] * (count - 1),
        in_specs=[VMEM] * 2 + [ANY] * len(deps),
        out_specs=[VMEM] * count,
        compiler_params=params(8),
        cost_estimate=cost(1),
        name="lag_blocks",
    )(forward, mirrored, *deps)


def side_by_side(pieces):
    rows, cq = pieces[0].shape

    def kernel(*refs):
        q = group_index()
        for k in range(INNER):
            refs[INNER][:, columns(q ^ k, cq)] = refs[k][...]
        refs[-1][...] = jnp.zeros(TOKEN, F32)

    return pl.pallas_call(
        kernel,
        out_shape=[shape((rows, INNER * cq), pieces[0].dtype), shape(TOKEN, F32)],
        in_specs=[VMEM] * INNER,
        out_specs=[VMEM] * 2,
        compiler_params=params(8),
        cost_estimate=cost(1),
        name="side_by_side",
    )(*pieces)


def placed_by_source(pieces, q):
    result = jnp.zeros((INNER,) + pieces[0].shape, pieces[0].dtype)
    for k, piece in enumerate(pieces):
        result = lax.dynamic_update_index_in_dim(result, piece, q ^ k, 0)
    return result


def by_member(value, q):
    return [lax.dynamic_index_in_dim(value, q ^ k, 0, keepdims=False) for k in range(INNER)]


def pick_member(pieces, q, member):
    result = pieces[0]
    for k in range(1, INNER):
        result = jnp.where((q ^ k) == member, pieces[k], result)
    return result


def body(grad_out, saved_in, filter_taps, skip_gain, projection):
    rows, width = grad_out.shape
    taps = filter_taps.shape[0]
    n_seq, n_ch = lax.axis_size("seq"), lax.axis_size("ch")
    outer = n_seq // INNER
    cq = width // INNER
    span = INNER * rows
    window = span + 2 * rows
    seq = lax.axis_index("seq")
    q, z = seq % INNER, seq // INNER
    const = transforms(rows)
    special = outer == 4 and n_ch == 2

    if special:
        shift = lambda v, table: lax.ppermute(
            v, "seq", [(INNER * a + i, INNER * b + i) for a, b in table for i in range(INNER)]
        )
        near = shift(projection, [(0, 1), (1, 0), (2, 3), (3, 2)])
        mid = shift(projection, [(1, 2), (2, 1)])

    singles = [(k,) for k in range(INNER)]
    grads = spread(quarters(grad_out, singles))
    mirrored = mirror_ch(quarters(filter_taps, [(0,)], reverse=True)[0])
    quarter = own_quarter(filter_taps, mirrored, skip_gain.reshape(1, width))

    final, initial = pick_member(grads, q, INNER - 1), pick_member(grads, q, 0)
    before = lax.ppermute(final, "seq", [(i, i + INNER) for i in range(n_seq - INNER)])
    after = lax.ppermute(initial, "seq", [(i + INNER, i) for i in range(n_seq - INNER)])
    near_ones, far = (), ()
    if special:
        near_ones = (near, mid)
        far_ends = shift(mid, [(1, 0), (2, 3)])
        far_mid = shift(near, [(2, 1), (1, 2)])
        far = (far_mid, far_ends)
        last = shift(far_mid, [(1, 0), (2, 3)])
    input_own, input_near, input_far = quarters(saved_in, [(0,), (1,), (2, 3)], (grads[2],))
    input_far = swap_seq(input_far, 2)
    inputs = [input_own, swap_seq(input_near, 1), input_far[0], swap_seq(input_far[1], 1)]
    spectrum, conv = filtered(grads, before, after, *quarter, const, (input_far,), near_ones)

    conv2 = swap_seq(conv, 2)
    conv1 = swap_seq(conv, 1)
    scale = 2.0 / window / math.sqrt(rows * n_seq)
    forward, turned, token = correlations(inputs, spectrum, const, scale, far)
    conv3 = [swap_seq(half, 1) for half in halves_after(conv2, token)]
    conv_parts = [conv, conv1, conv2, *conv3]

    mirrored = lax.ppermute(
        turned,
        ("seq", "ch"),
        [
            (s * n_ch + c, (s ^ (INNER - 1)) * n_ch + n_ch - 1 - c)
            for s in range(n_seq)
            for c in range(n_ch)
        ],
    )
    if special:
        x2 = [("end", far_ends), ("mid", far_mid)]
        x3 = [("end", last), ("mid", mid)]
        sent = lambda late, soon: [("early_" + w, block) for w, block in late] + [("late", soon)]
        kept = lambda late, soon: [("late_" + w, block) for w, block in late] + [("early", soon)]
        first, token = project(conv_parts, sent(x2, projection), BF16, (token,))
        got = mirror_ch(first)
        own, token = project(conv_parts, kept(x2, projection), F32, (token,))
        lag_own, *lag_sent = lag_blocks(forward, mirrored, outer, ())
        second, token = project(conv_parts, sent(x3, near), BF16, (token, lag_own))
        got2 = mirror_ch(second)
        lag_got = [swap_seq(block, INNER * (k + 1)) for k, block in enumerate(lag_sent)]
        moved = spread(summed_rows(own, got, []))
        own2, token = project(conv_parts, kept(x3, near), F32, (token,))
        moved2 = spread(summed_rows(own2, got2, [lag_own] + lag_got))
        grad_in, filter_grad = assembled(moved, moved2, width)
    else:
        groups = [[INNER * a + i for a in range(outer)] for i in range(INNER)]
        proj_all = lax.all_gather(projection, "seq", axis=0, axis_index_groups=groups)
        conv_all = placed_by_source([conv, conv1, conv2, jnp.concatenate(conv3, 0)], q)
        partial_value = lax.dot_general(
            conv_all.transpose(1, 0, 2).reshape(span, width),
            proj_all.reshape(-1, width),
            (((1,), (1,)), ((), ())),
            preferred_element_type=F32,
        )
        total = lax.psum_scatter(
            partial_value.astype(BF16), "ch", scatter_dimension=1, tiled=True
        )
        o_rows = projection.shape[0]
        moved = spread(by_member(total.reshape(INNER, rows, -1), q))
        stacked = placed_by_source(moved, q).reshape(INNER, rows, -1, o_rows)
        grad_in = stacked.transpose(1, 2, 0, 3).reshape(rows, width)

        summed = lax.psum_scatter(
            forward + mirrored.astype(F32), "seq", scatter_dimension=0, tiled=True, axis_index_groups=groups
        )
        lag_pieces = by_member(summed.reshape(INNER, -1, cq), q)
        filter_grad, _ = side_by_side(spread(lag_pieces))
    return (grad_in, filter_grad)


def solution(mesh):
    placed = (P("seq", "ch"), P("seq", "ch"), P(None, "ch"), P("ch"), P("seq", "ch"))
    return jax.shard_map(
        body,
        mesh=mesh,
        in_specs=placed,
        out_specs=(P("seq", "ch"), P("seq", "ch")),
        check_vma=False,
    )
```
